32 devices in a mesh: seq: 8 (over y, x, core), head: 4 (over z).
Axes of the slice: x: 2, y: 2, z: 4, core: 2. Of those that a mesh axis runs over, the one named last changes fastest.
Arguments:
- query_vectors: bfloat16 [4096, 4096], P('seq', 'head'), may hold values from -4.375 to 4.375
- key_vectors: bfloat16 [4096, 4096], P('seq', 'head'), may hold values from -4.375 to 4.375
- value_vectors: bfloat16 [4096, 4096], P('seq', 'head'), may hold values from -8 to 8
- upstream: bfloat16 [4096, 4096], P('seq', 'head'), may hold values from -6 to 6
- out_weight: bfloat16 [4096, 4096], P('head', 'seq'), may hold values from -0.09375 to 0.09375
- gate_logit: float32 [32], P('head'), may hold values from -2 to 2
- document_ids: int32 [8], replicated, may hold values from 0 to 2, as said below
- valid_lengths: int32 [8], replicated, may hold values from 64 to 512, as said below
Outputs:
- mixed: bfloat16 [4096, 4096], P('seq', 'head')
- grad_queries: bfloat16 [4096, 4096], P('seq', 'head')
- grad_keys: bfloat16 [4096, 4096], P('seq', 'head')
- grad_values: bfloat16 [4096, 4096], P('seq', 'head')
The draws below stay inside these ranges and needn't reach their ends.
Inputs may be any that keep to these rules, and one draw needn't show every extreme that they name: `document_ids`: never falling; every document spans 1 to 4 consecutive segments, and one spans exactly 4. `valid_lengths`: every segment but the last of its document is full; the last segment of some document holds 64 tokens.
All inputs are finite; a program needn't handle non-finite values.
Results may differ from the reference program's by a relative error of at most 0.012.
Values may be sent and summed in bfloat16 or wider, within the bound.
A program may use at most 128 MiB of HBM per device.

```python
import jax
import jax.numpy as jnp
from jax import lax

D = 4096
HEADS = 32
HD = 128
SEG = 512
NSEG = 8
TOKENS = 4096
DOCS = 3


def document_layout(key):
    half_count = NSEG // 2
    cut_points = jax.random.permutation(jax.random.fold_in(key, 21), half_count - 1)[:DOCS - 2] + 1
    short_starts = jnp.zeros((half_count,), jnp.int32).at[0].set(1).at[cut_points].set(1)
    short_docs = (jnp.cumsum(short_starts) - 1).astype(jnp.int32)
    bounds = jnp.concatenate([jnp.zeros((1,), jnp.int32), jnp.sort(cut_points).astype(jnp.int32), jnp.full((1,), half_count, jnp.int32)])
    insert_rank = jax.random.randint(jax.random.fold_in(key, 22), (), 0, DOCS, dtype=jnp.int32)
    long_begin = bounds[insert_rank]
    segment_index = jnp.arange(NSEG, dtype=jnp.int32)
    before_docs = short_docs[jnp.clip(segment_index, 0, half_count - 1)]
    after_docs = short_docs[jnp.clip(segment_index - half_count, 0, half_count - 1)] + 1
    doc_numbers = jnp.where(segment_index < long_begin, before_docs, jnp.where(segment_index < long_begin + half_count, insert_rank, after_docs)).astype(jnp.int32)
    long_last = long_begin + half_count - 1
    return (doc_numbers, long_last)


def draw_document_ids(key, part):
    doc_numbers, long_last = document_layout(key)
    return doc_numbers


def draw_valid_lengths(key, part):
    doc_numbers, long_last = document_layout(key)
    key = jax.random.fold_in(key, 3)
    tails = jax.random.randint(key, (NSEG,), SEG // 8, SEG + 1, dtype=jnp.int32)
    is_last = doc_numbers != jnp.concatenate([doc_numbers[1:], jnp.full((1,), -1, jnp.int32)])
    lengths = jnp.where(is_last, tails, SEG).astype(jnp.int32)
    return lengths.at[long_last].set(SEG // 8)


def draw_query_vectors(key, part):
    key = jax.random.fold_in(key, 1)
    base = jnp.clip(jax.random.normal(key, (TOKENS, HEADS * HD), jnp.float32), -4.375, 4.375)
    return base.astype(jnp.bfloat16)


def draw_key_vectors(key, part):
    key = jax.random.fold_in(key, 2)
    offsets = jax.random.uniform(jax.random.fold_in(key, 7), (NSEG, 1, HEADS, 1), jnp.float32, -2.0, 2.0)
    offsets = jnp.broadcast_to(offsets, (NSEG, SEG, HEADS, HD)).reshape(TOKENS, HEADS * HD)
    base = jax.random.normal(key, (TOKENS, HEADS * HD), jnp.float32)
    base = jnp.clip(base + offsets, -4.375, 4.375)
    return base.astype(jnp.bfloat16)


def draw_value_vectors(key, part):
    key = jax.random.fold_in(key, 5)
    shift = jax.random.normal(jax.random.fold_in(key, 2), (NSEG, 1, HEADS * HD), jnp.float32)
    noise = jax.random.normal(jax.random.fold_in(key, 1), (NSEG, SEG, HEADS * HD), jnp.float32)
    return jnp.clip(noise + shift, -8.0, 8.0).reshape(TOKENS, HEADS * HD).astype(jnp.bfloat16)


def level_of(stream_key, dims, shards, least, top_value):
    def one(axis_at, blocks):
        steps = jax.random.uniform(jax.random.fold_in(jax.random.fold_in(stream_key, 6), axis_at), (blocks,), jnp.float32, least / len(shards), top_value / len(shards))
        return jnp.repeat(jnp.exp(steps), dims[axis_at] // blocks).reshape((-1,) + (1,) * (len(dims) - axis_at - 1))

    gain = one(*shards[0])
    for cut in shards[1:]:
        gain = gain * one(*cut)
    return gain


def normal_values(key, shape, spread, reach, shards=(), kind=jnp.bfloat16):
    drawn = jax.random.normal(key, shape, jnp.float32) * spread
    if len(shards) > 0:
        drawn = level_of(key, shape, shards, -0.22, 0.18) * drawn
    return jnp.clip(drawn, min=-reach, max=reach).astype(kind)


def setup_inputs(seed: int = 0) -> dict:
    key_list = jax.random.split(jax.random.key(seed), 9)
    query_vectors = draw_query_vectors(jax.random.fold_in(key_list[8], 71), 0)
    key_vectors = draw_key_vectors(jax.random.fold_in(key_list[8], 71), 0)
    value_vectors = draw_value_vectors(jax.random.fold_in(key_list[8], 71), 0)
    upstream = normal_values(key_list[3], (TOKENS, D), 1.0, 6.0, ((0, 8), (1, 4)))
    out_weight = normal_values(key_list[4], (HEADS * HD, D), (HEADS * HD) ** -0.5, 0.09375, ((0, 4), (1, 8)))
    gate_logit = jnp.clip(jax.random.uniform(key_list[5], (HEADS,), jnp.float32, -2.0, 2.0) * level_of(key_list[5], (HEADS,), ((0, 4),), -0.4, 0.0), -2.0, 2.0)
    document_ids = draw_document_ids(jax.random.fold_in(key_list[8], 71), 0)
    valid_lengths = draw_valid_lengths(jax.random.fold_in(key_list[8], 71), 0)
    return dict(query_vectors=query_vectors, key_vectors=key_vectors, value_vectors=value_vectors, upstream=upstream, out_weight=out_weight, gate_logit=gate_logit, document_ids=document_ids, valid_lengths=valid_lengths)


HIGHEST = lax.Precision.HIGHEST

def feature_map(values_in):
    return jnp.where(values_in > 0, values_in + 1.0, jnp.exp(jnp.minimum(values_in, 0.0)))

def segment_attention(query_block, key_block, value_block, memory, normalizer, gate_value, valid_count):
    length = query_block.shape[0]
    half_rows = length // 2
    score_scale = query_block.shape[1] ** (-0.5)
    position = jnp.arange(length)
    live_rows = (position < valid_count).astype(query_block.dtype)
    pieces = []
    for start_row, key_count in ((0, half_rows), (half_rows, length)):
        query_rows = query_block[start_row:start_row + half_rows]
        scores = jnp.dot(query_rows, key_block[:key_count].T, precision=HIGHEST) * score_scale
        allowed = (position[None, :key_count] <= position[start_row:start_row + half_rows, None]) & (position[None, :key_count] < valid_count)
        scores = jnp.where(allowed, scores, -1e+30)
        row_max = lax.optimization_barrier(jnp.max(scores, axis=1, keepdims=True))
        weights = jnp.exp(scores - row_max)
        weights = weights / lax.optimization_barrier(jnp.sum(weights, axis=1, keepdims=True))
        pieces.append(jnp.dot(weights, value_block[:key_count], precision=HIGHEST))
    local_out = jnp.concatenate(pieces, axis=0)
    lifted = feature_map(query_block)
    numerator = jnp.dot(lifted, memory, precision=HIGHEST)
    denominator = 1.0 + jnp.dot(lifted, normalizer, precision=HIGHEST)
    recalled = numerator / denominator[:, None]
    return (gate_value * recalled + (1.0 - gate_value) * local_out) * live_rows[:, None]

def memory_terms(key_block, value_block, valid_count):
    live_rows = (jnp.arange(key_block.shape[0]) < valid_count).astype(key_block.dtype)
    lifted = feature_map(key_block) * live_rows[:, None]
    return (jnp.dot(lifted.T, value_block, precision=HIGHEST), lax.optimization_barrier(jnp.sum(lifted, axis=0)))

def combine(earlier, later):
    keep_part = 1.0 - later[0]
    return (jnp.maximum(earlier[0], later[0]), later[1] + keep_part * earlier[1], later[2] + keep_part * earlier[2])

def segment_step(query_block, key_block, value_block, memory, normalizer, gate_value, valid_count, grad_out):

    def attend(query_full, key_full, value_full, memory_full, normalizer_full):
        return segment_attention(query_full, key_full, value_full, memory_full, normalizer_full, gate_value, valid_count)
    result, backward = jax.vjp(attend, query_block.astype(jnp.float32), key_block.astype(jnp.float32), value_block.astype(jnp.float32), memory, normalizer)
    return (result,) + tuple(backward(grad_out.astype(jnp.float32)))

def head_memory(key_seg, value_seg, valid_count):

    def single(key_head, value_head):
        return memory_terms(key_head.astype(jnp.float32), value_head.astype(jnp.float32), valid_count)
    return jax.vmap(single)(key_seg, value_seg)

def memory_step(key_seg, value_seg, valid_count, grad_mem, grad_norm):

    def single(key_head, value_head, mem_head, norm_head):

        def terms_of(key_full, value_full):
            return memory_terms(key_full, value_full, valid_count)
        _, backward = jax.vjp(terms_of, key_head.astype(jnp.float32), value_head.astype(jnp.float32))
        return backward((mem_head, norm_head))
    return jax.vmap(single)(key_seg, value_seg, grad_mem, grad_norm)

def reference(query_vectors, key_vectors, value_vectors, upstream, out_weight, gate_logit, document_ids, valid_lengths):

    def split_heads(array):
        return array.reshape(NSEG, SEG, HEADS, HD).transpose(0, 2, 1, 3)

    def merge_heads(array):
        return array.transpose(0, 2, 1, 3).reshape(NSEG * SEG, HEADS * HD)
    query_heads = split_heads(query_vectors)
    key_heads = split_heads(key_vectors)
    value_heads = split_heads(value_vectors)
    gate_values = jax.nn.sigmoid(gate_logit)

    def segment_memory(inputs):
        return head_memory(inputs[0], inputs[1], inputs[2])
    kv_terms, key_sums = lax.map(segment_memory, (key_heads, value_heads, valid_lengths))
    previous = jnp.concatenate([jnp.full((1,), -1, jnp.int32), document_ids[:-1]])
    starts = (document_ids != previous).astype(jnp.float32)
    keep = 1.0 - starts
    identity = (jnp.zeros((), jnp.float32), jnp.zeros_like(kv_terms[0]), jnp.zeros_like(key_sums[0]))

    def carry_step(running, element):
        return (combine(running, element), running)
    _, before = lax.scan(carry_step, identity, (starts, kv_terms, key_sums))
    memory_prev = before[1] * keep[:, None, None, None]
    normalizer_prev = before[2] * keep[:, None, None]
    grad_attn = jnp.dot(upstream, out_weight.T, preferred_element_type=jnp.float32).astype(jnp.bfloat16)
    grad_heads = split_heads(grad_attn)

    def segment_pass(inputs):
        query_seg, key_seg, value_seg, memory_seg, normalizer_seg, valid_count, grad_seg = inputs
        outcome = jax.vmap(segment_step, in_axes=(0, 0, 0, 0, 0, 0, None, 0))(query_seg, key_seg, value_seg, memory_seg, normalizer_seg, gate_values, valid_count, grad_seg)
        return (outcome[0].astype(jnp.bfloat16), outcome[1].astype(jnp.bfloat16)) + tuple(outcome[2:])
    attn_out, grad_query, grad_key_local, grad_value_local, grad_memory, grad_normalizer = lax.map(segment_pass, (query_heads, key_heads, value_heads, memory_prev, normalizer_prev, valid_lengths, grad_heads))
    elements = (starts, grad_memory * keep[:, None, None, None], grad_normalizer * keep[:, None, None])
    _, after = lax.scan(carry_step, identity, elements, reverse=True)

    def segment_back(inputs):
        return memory_step(inputs[0], inputs[1], inputs[2], inputs[3], inputs[4])
    grad_key_memory, grad_value_memory = lax.map(segment_back, (key_heads, value_heads, valid_lengths, after[1], after[2]))
    mixed = jnp.dot(merge_heads(attn_out), out_weight, preferred_element_type=jnp.float32).astype(jnp.bfloat16)
    grad_keys = merge_heads((grad_key_local + grad_key_memory).astype(jnp.bfloat16))
    grad_values = merge_heads((grad_value_local + grad_value_memory).astype(jnp.bfloat16))
    return (mixed, merge_heads(grad_query), grad_keys, grad_values)
```

```python
import functools

import jax
import jax.numpy as jnp
from jax import lax
from jax.experimental import pallas as pl
from jax.experimental.pallas import tpu as pltpu
from jax.sharding import PartitionSpec as P

F32 = jnp.float32
BF16 = jnp.bfloat16
EXT = 16
PARAMS = pltpu.CompilerParams(vmem_limit_bytes=40 * 1024 * 1024)

SMEM = pl.BlockSpec(memory_space=pltpu.SMEM)


def lift(x):
    return jnp.where(x > 0, x + 1.0, jnp.exp(jnp.minimum(x, 0.0)))


def lift_slope(x):
    return jnp.where(x > 0, 1.0, jnp.exp(jnp.minimum(x, 0.0)))


def dot(a, b, ca, cb):
    return lax.dot_general(a, b, (((ca,), (cb,)), ((), ())), preferred_element_type=F32)


def row_mask(rows, valid, first=0):
    return lax.broadcasted_iota(jnp.int32, (rows, 1), 0) + first < valid


def with_ones(v):
    return jnp.concatenate([v, jnp.ones((v.shape[0], EXT), v.dtype)], axis=1)


def state_kernel(valid_ref, k_ref, v_ref, out_ref):
    seg, hd = k_ref.shape
    live = row_mask(seg, valid_ref[0])
    lifted = jnp.where(live, lift(k_ref[...].astype(F32)), 0.0).astype(BF16)
    out_ref[0] = dot(with_ones(v_ref[...]), lifted, 0, 0).astype(BF16)


def total_state(weight_ref, all_ref):
    total = jnp.zeros(all_ref.shape[2:], F32)
    for t in range(all_ref.shape[0]):
        total = total + jnp.where(weight_ref[t] > 0, all_ref[t, 0].astype(F32), 0.0)
    return total


def forward_kernel(valid_ref, weight_ref, gate_ref, q_ref, k_ref, v_ref, all_ref, attn_ref, p_ref, mem_ref):
    seg, hd = q_ref.shape
    half = seg // 2
    valid = valid_ref[0]
    gate = gate_ref[pl.program_id(0)]
    mem = total_state(weight_ref, all_ref).astype(BF16)
    mem_ref[0] = mem
    scale = hd ** -0.5
    lifted = lift(q_ref[...].astype(F32)).astype(BF16)
    recall = dot(lifted, mem, 1, 1)
    recalled = recall[:, :hd] / (1.0 + recall[:, hd:hd + 1])
    p_ref[0, :half, half:] = jnp.zeros((half, seg - half), BF16)
    for first, count in ((0, half), (half, seg)):
        rows = slice(first, first + half)
        s = dot(q_ref[rows, :], k_ref[:count, :], 1, 1) * scale
        r = lax.broadcasted_iota(jnp.int32, (half, count), 0) + first
        c = lax.broadcasted_iota(jnp.int32, (half, count), 1)
        s = jnp.where((c <= r) & (c < valid), s, -1e30)
        e = jnp.exp(s - jnp.max(s, axis=1, keepdims=True))
        p = (e / jnp.sum(e, axis=1, keepdims=True)).astype(BF16)
        p_ref[0, rows, :count] = p
        local = dot(p, v_ref[:count, :], 1, 0)
        attn = gate * recalled[rows] + (1.0 - gate) * local
        attn_ref[rows, :] = jnp.where(row_mask(half, valid, first), attn, 0.0).astype(BF16)


def recall_back(lifted, mem, da, gate):
    hd = lifted.shape[1]
    recall = dot(lifted, mem, 1, 1)
    inv = 1.0 / (1.0 + recall[:, hd:hd + 1])
    dnum = da * (gate * inv)
    dden = -jnp.sum(dnum * recall[:, :hd], axis=1, keepdims=True) * inv
    high = dden.astype(BF16).astype(F32)
    lane = lax.broadcasted_iota(jnp.int32, (lifted.shape[0], EXT), 1)
    tail = jnp.where(lane == 0, high, jnp.where(lane == 1, dden - high, 0.0))
    return jnp.concatenate([dnum.astype(BF16), tail.astype(BF16)], axis=1)


def grad_state_kernel(valid_ref, gate_ref, q_ref, mem_ref, da_ref, out_ref):
    seg, hd = q_ref.shape
    gate = gate_ref[pl.program_id(0)]
    live = row_mask(seg, valid_ref[0])
    da = jnp.where(live, da_ref[...].astype(F32), 0.0)
    lifted = lift(q_ref[...].astype(F32)).astype(BF16)
    ext = recall_back(lifted, mem_ref[0], da, gate)
    out = dot(ext, lifted, 0, 0)
    out_ref[0, :hd] = out[:hd].astype(BF16)
    norm = out[hd:hd + 1] + out[hd + 1:hd + 2]
    out_ref[0, hd:] = jnp.broadcast_to(norm, (EXT, hd)).astype(BF16)


def backward_kernel(valid_ref, gate_ref, q_ref, k_ref, v_ref, p_ref, mem_ref, da_ref, dq_ref, dk_ref, dv_ref):
    seg, hd = q_ref.shape
    gate = gate_ref[pl.program_id(0)]
    live = row_mask(seg, valid_ref[0])
    da = jnp.where(live, da_ref[...].astype(F32), 0.0)
    q32 = q_ref[...].astype(F32)
    lifted = lift(q32).astype(BF16)
    ext = recall_back(lifted, mem_ref[0], da, gate)
    dlifted = dot(ext, mem_ref[0], 1, 0)
    do = ((1.0 - gate) * da).astype(BF16)
    p = p_ref[0]
    dv_ref[...] = dot(p, do, 0, 0)
    dp = dot(do, v_ref[...], 1, 1)
    p32 = p.astype(F32)
    weighted = p32 * dp
    ds = (weighted - p32 * jnp.sum(weighted, axis=1, keepdims=True)).astype(BF16)
    scale = hd ** -0.5
    dk_ref[...] = dot(ds, q_ref[...], 0, 0) * scale
    dq = dot(ds, k_ref[...], 1, 0) * scale + dlifted * lift_slope(q32)
    dq_ref[...] = dq.astype(BF16)


def final_kernel(valid_ref, weight_ref, k_ref, v_ref, all_ref, dk_ref, dv_ref, outk_ref, outv_ref):
    seg, hd = k_ref.shape
    live = row_mask(seg, valid_ref[0])
    total = total_state(weight_ref, all_ref)
    row = lax.broadcasted_iota(jnp.int32, total.shape, 0)
    total = jnp.where(row <= hd, total, 0.0).astype(BF16)
    k32 = k_ref[...].astype(F32)
    dlifted = dot(with_ones(v_ref[...]), total, 1, 0)
    slope = jnp.where(live, lift_slope(k32), 0.0)
    outk_ref[...] = (dk_ref[...] + dlifted * slope).astype(BF16)
    lifted = jnp.where(live, lift(k32), 0.0).astype(BF16)
    outv_ref[...] = (dv_ref[...] + dot(lifted, total[:hd], 1, 1)).astype(BF16)


def product_kernel(a_ref, w_ref, out_ref):
    out_ref[0] = dot(a_ref[...], w_ref[0], 1, 0).astype(BF16)


def grad_product_kernel(u_ref, w_ref, out_ref, acc_ref):
    t = pl.program_id(0)
    part = dot(u_ref[0], w_ref[0], 1, 1)

    @pl.when(t == 0)
    def _():
        acc_ref[...] = part

    @pl.when(t > 0)
    def _():
        acc_ref[...] += part

    @pl.when(t == pl.num_programs(0) - 1)
    def _():
        out_ref[...] = acc_ref[...].astype(BF16)


def cost(flops, nbytes):
    return pl.CostEstimate(flops=int(flops), bytes_accessed=int(nbytes), transcendentals=0)


def per_device(q, k, v, upstream, out_weight, gate_logit, document_ids, valid_lengths):
    heads = gate_logit.shape[0]
    seg, width = q.shape
    hd = width // heads
    nseq, nhead = lax.axis_size("seq"), lax.axis_size("head")
    me = lax.axis_index("seq")
    gates = jax.nn.sigmoid(gate_logit)
    valid = lax.dynamic_slice(valid_lengths, (me,), (1,))
    same = document_ids == lax.dynamic_slice(document_ids, (me,), (1,))
    index = jnp.arange(nseq, dtype=jnp.int32)
    earlier = (same & (index < me)).astype(jnp.int32)
    later = (same & (index > me)).astype(jnp.int32)

    col = pl.BlockSpec((seg, hd), lambda h: (0, h))
    state = pl.BlockSpec((1, hd + EXT, hd), lambda h: (h, 0, 0))
    states = pl.BlockSpec((nseq, 1, hd + EXT, hd), lambda h: (0, h, 0, 0))
    square = pl.BlockSpec((1, seg, seg), lambda h: (h, 0, 0))
    state_shape = jax.ShapeDtypeStruct((heads, hd + EXT, hd), BF16)
    big16 = jax.ShapeDtypeStruct((seg, width), BF16)
    big32 = jax.ShapeDtypeStruct((seg, width), F32)
    unit = 2.0 * heads * seg * hd

    kv = pl.pallas_call(
        state_kernel, grid=(heads,), in_specs=[SMEM, col, col], out_specs=state,
        out_shape=state_shape, compiler_params=PARAMS, name="states",
        cost_estimate=cost(unit * hd, 4 * seg * width),
    )(valid, k, v)
    kv_all = lax.all_gather(kv, "seq")
    w_all = lax.all_gather(out_weight, "seq")
    u_all = lax.all_gather(upstream, "head")

    attn, p, mem = pl.pallas_call(
        forward_kernel, grid=(heads,), in_specs=[SMEM, SMEM, SMEM, col, col, col, states],
        out_specs=[col, square, state],
        out_shape=[big16, jax.ShapeDtypeStruct((heads, seg, seg), BF16), state_shape],
        compiler_params=PARAMS, name="forward",
        cost_estimate=cost(unit * (3 * seg + hd), 8 * seg * width + 2 * heads * seg * seg),
    )(valid, earlier, gates, q, k, v, kv_all)

    wcols = out_weight.shape[1]
    per = nseq // nhead
    full = pl.BlockSpec((seg, width), lambda t: (0, 0))
    wspec = pl.BlockSpec((1, width, wcols), lambda t: (t, 0, 0))
    partspec = pl.BlockSpec((1, seg, wcols), lambda t: (t // per, 0, t % per))
    terms = pl.pallas_call(
        product_kernel, grid=(nseq,), in_specs=[full, wspec], out_specs=partspec,
        out_shape=jax.ShapeDtypeStruct((nhead, seg, wcols * per), BF16),
        compiler_params=PARAMS, name="project",
        cost_estimate=cost(2.0 * seg * width * wcols * nseq, 2 * (width + seg) * wcols * nseq),
    )(attn, w_all)
    mixed = lax.psum_scatter(terms, "head", scatter_dimension=0, tiled=False)

    da = pl.pallas_call(
        grad_product_kernel, grid=(nseq,), in_specs=[partspec, wspec], out_specs=full,
        out_shape=big16, scratch_shapes=[pltpu.VMEM((seg, width), F32)],
        compiler_params=PARAMS, name="grad_attn",
        cost_estimate=cost(2.0 * seg * width * wcols * nseq, 2 * (width + seg) * wcols * nseq),
    )(u_all, w_all)
    gm = pl.pallas_call(
        grad_state_kernel, grid=(heads,), in_specs=[SMEM, SMEM, col, state, col],
        out_specs=state, out_shape=state_shape, compiler_params=PARAMS, name="grad_states",
        cost_estimate=cost(unit * hd * 2, 4 * seg * width),
    )(valid, gates, q, mem, da)
    gm_all = lax.all_gather(gm, "seq")
    dq, dk, dv = pl.pallas_call(
        backward_kernel, grid=(heads,),
        in_specs=[SMEM, SMEM, col, col, col, square, state, col], out_specs=[col, col, col],
        out_shape=[big16, big32, big32], compiler_params=PARAMS, name="backward",
        cost_estimate=cost(unit * (4 * seg + 2 * hd), 18 * seg * width + 2 * heads * seg * seg),
    )(valid, gates, q, k, v, p, mem, da)
    gk, gv = pl.pallas_call(
        final_kernel, grid=(heads,), in_specs=[SMEM, SMEM, col, col, states, col, col],
        out_specs=[col, col], out_shape=[big16, big16], compiler_params=PARAMS, name="final",
        cost_estimate=cost(unit * hd * 2, 16 * seg * width),
    )(valid, later, k, v, gm_all, dk, dv)
    return mixed, dq, gk, gv


def solution(mesh):
    spec = P("seq", "head")
    return jax.shard_map(
        per_device,
        mesh=mesh,
        in_specs=(spec, spec, spec, spec, P("head", "seq"), P("head"), P(), P()),
        out_specs=(spec, spec, spec, spec),
        check_vma=False,
    )
```

```python
import functools

import jax
import jax.numpy as jnp
from jax import lax
from jax.experimental import pallas as pl
from jax.experimental.pallas import tpu as pltpu
from jax.sharding import PartitionSpec as P

F32 = jnp.float32
BF16 = jnp.bfloat16
EXT = 16
MESH = pl.DeviceIdType.MESH


def lift(x):
    return jnp.where(x > 0, x + 1.0, jnp.exp(jnp.minimum(x, 0.0)))


def lift_slope(x):
    return jnp.where(x > 0, 1.0, jnp.exp(jnp.minimum(x, 0.0)))


def dot(a, b, ca, cb):
    return lax.dot_general(a, b, (((ca,), (cb,)), ((), ())), preferred_element_type=F32)


def row_mask(rows, valid, first=0):
    return lax.broadcasted_iota(jnp.int32, (rows, 1), 0) + first < valid


def with_ones(v):
    return jnp.concatenate([v, jnp.ones((v.shape[0], EXT), v.dtype)], axis=1)


def kernel(
    nseq, nhead, heads,
    valid_ref, doc_ref, gate_ref, q_ref, k_ref, v_ref, u_ref, w_ref,
    mixed_ref, dq_ref, gk_ref, gv_ref,
    wall, uall, terms, parts, probs, acc, lifted_ref, recalled_ref, ginv_ref,
    dk_ref, dv_ref, attn_ref, da_ref, mem_ref, kv_own, kv_in, gm_own, gm_in,
    w_send, w_pass, w_recv, u_send, u_recv, kv_send, kv_recv, gm_send, gm_recv,
    p_send, p_recv, own_sem,
):
    seg, width = q_ref.shape
    hd = width // heads
    half = seg // 2
    span = nseq // 2
    chips = nseq // 2
    per = nseq // nhead
    wcols = w_ref.shape[1]
    scale = hd ** -0.5
    me = lax.axis_index("seq")
    z = lax.axis_index("head")
    chip, core = me // 2, me % 2
    partner = chip * 2 + 1 - core
    has_left, has_right = z > 0, z < nhead - 1

    barrier = pltpu.get_barrier_semaphore()
    for d in range(1, nseq):
        pl.semaphore_signal(
            barrier, inc=1, device_id=((me + d) % nseq, z), device_id_type=MESH
        )

    for d in range(1, nhead):
        pl.semaphore_signal(
            barrier, inc=1, device_id=(me, (z + d) % nhead), device_id_type=MESH
        )
    pl.semaphore_wait(barrier, nseq + nhead - 2)

    def remote(src, dst, send, recv, seq, head):
        return pltpu.make_async_remote_copy(
            src_ref=src, dst_ref=dst, send_sem=send, recv_sem=recv,
            device_id=(seq, head), device_id_type=MESH,
        )

    def u_copy(way, hop):
        block = z - hop if way == 0 else z + hop
        to = z + 1 if way == 0 else z - 1
        src = u_ref if hop == 0 else uall.at[block]
        return remote(src, uall.at[block], u_send.at[way, hop], u_recv.at[block], me, to)

    def u_sends(way, hop):
        if way == 0:
            return has_right & (z >= hop)
        return has_left & (z + hop <= nhead - 1)

    def u_wait(block):
        remote(u_ref, uall.at[block], u_send.at[0, 0], u_recv.at[block], me, z).wait_recv()

    def u_arrived(hop):
        for way in range(2):
            block = z - hop if way == 0 else z + hop
            there = (z >= hop) if way == 0 else (z + hop <= nhead - 1)

            @pl.when(there)
            def _():
                u_wait(block)

            if hop < nhead - 1:

                @pl.when(u_sends(way, hop))
                def _():
                    u_copy(way, hop).start()

    for way in range(2):

        @pl.when(u_sends(way, 0))
        def _():
            u_copy(way, 0).start()

    def w_to_partner(delta):
        block = ((chip - delta + chips) % chips) * 2 + core
        src = w_ref if delta == 0 else wall.at[block]
        return remote(src, wall.at[block], w_pass.at[delta], w_recv.at[block], partner, z)

    def w_to_chip(delta):
        to = ((chip + delta) % chips) * 2 + core
        return remote(w_ref, wall.at[me], w_send.at[delta], w_recv.at[me], to, z)

    def w_wait(block):
        remote(w_ref, wall.at[block], w_pass.at[0], w_recv.at[block], partner, z).wait_recv()

    w_to_partner(0).start()
    own_w = pltpu.make_async_copy(w_ref, wall.at[me], own_sem.at[0])
    own_w.start()
    own_u = pltpu.make_async_copy(u_ref, uall.at[z], own_sem.at[1])
    own_u.start()

    valid = valid_ref[me]
    live = row_mask(seg, valid)

    def lanes(h):
        return pl.ds(pl.multiple_of(h * hd, hd), hd)

    def gate_of(h):
        return 1.0 / (1.0 + jnp.exp(jnp.full((1, hd), -gate_ref[h], F32)))

    def over_heads(body):
        def step(h, carry):
            body(h)
            return carry

        lax.fori_loop(0, heads, step, 0)

    @over_heads
    def _(h):
        lifted = jnp.where(live, lift(k_ref[:, lanes(h)].astype(F32)), 0.0).astype(BF16)
        kv_own[h] = dot(with_ones(v_ref[:, lanes(h)]), lifted, 0, 0).astype(BF16)

    def kv_copy(d):
        return remote(
            kv_own, kv_in.at[d - 1], kv_send.at[d - 1], kv_recv.at[d - 1], (me + d) % nseq, z
        )

    def gm_copy(d):
        return remote(
            gm_own, gm_in.at[d - 1], gm_send.at[d - 1], gm_recv.at[d - 1],
            (me - d + nseq) % nseq, z,
        )

    for d in range(1, span):
        kv_copy(d).start()
    for delta in range(1, chips):
        w_to_chip(delta).start()

    @over_heads
    def _(h):
        keep = 1.0 - gate_of(h)
        probs[h, :half, half:] = jnp.zeros((half, seg - half), BF16)
        for first, count in ((0, half), (half, seg)):
            rows = slice(first, first + half)
            s = dot(q_ref[rows, lanes(h)], k_ref[:count, lanes(h)], 1, 1) * scale
            r = lax.broadcasted_iota(jnp.int32, (half, count), 0) + first
            c = lax.broadcasted_iota(jnp.int32, (half, count), 1)
            s = jnp.where((c <= r) & (c < valid), s, -1e30)
            e = jnp.exp(s - jnp.max(s, axis=1, keepdims=True))
            p = (e * (1.0 / jnp.sum(e, axis=1, keepdims=True))).astype(BF16)
            probs[h, rows, :count] = p
            acc[rows, lanes(h)] = keep * dot(p, v_ref[:count, lanes(h)], 1, 0)

    def weight_of(d, earlier):
        other = me - d if earlier else me + d
        inside = (other >= 0) if earlier else (other < nseq)
        index = (other + nseq) % nseq
        return (inside & (doc_ref[index] == doc_ref[me])).astype(F32)

    for d in range(1, span):
        kv_copy(d).wait_recv()

    def total_state(slots, earlier, h):
        total = jnp.zeros((hd + EXT, hd), F32)
        for d in range(1, span):
            total = total + weight_of(d, earlier) * slots[d - 1, h].astype(F32)
        return total

    @over_heads
    def _(h):
        gate = gate_of(h)
        mem = total_state(kv_in, True, h).astype(BF16)
        mem_ref[h] = mem
        lifted = lift(q_ref[:, lanes(h)].astype(F32)).astype(BF16)
        lifted_ref[:, lanes(h)] = lifted
        recall = dot(lifted, mem, 1, 1)
        inv = 1.0 / (1.0 + recall[:, hd:hd + 1])
        recalled = recall[:, :hd] * inv
        recalled_ref[:, lanes(h)] = recalled.astype(BF16)
        ginv_ref[:, lanes(h)] = jnp.where(live, gate * inv, 0.0)
        attn = gate * recalled + acc[:, lanes(h)]
        attn_ref[:, lanes(h)] = jnp.where(live, attn, 0.0).astype(BF16)

    def p_copy(block):
        owner, sub = block // per, block % per
        return remote(
            terms.at[block], parts.at[z, sub], p_send.at[block], p_recv.at[z, sub], me, owner
        )

    def project(block):
        terms[block] = dot(attn_ref[...], wall[block], 1, 0).astype(BF16)

        @pl.when(block // per != z)
        def _():
            p_copy(block).start()

    own_w.wait()
    project(me)
    w_wait(partner)
    project(partner)
    for delta in range(1, chips):
        base = ((chip - delta + chips) % chips) * 2
        w_wait(base + core)
        w_to_partner(delta).start()
        if delta < nhead - 1:
            u_arrived(delta)
        project(base + core)
        w_wait(base + 1 - core)
        project(base + 1 - core)

    def grad_product(block):
        for sub in range(per):
            acc[...] += dot(
                uall[block, :, sub * wcols:(sub + 1) * wcols], wall[block * per + sub], 1, 1
            )

    own_u.wait()
    acc[...] = jnp.zeros_like(acc)
    grad_product(z)
    for hop in range(1, nhead):
        if hop >= min(chips, nhead - 1):
            u_arrived(hop)
        for way in range(2):
            there = (z >= hop) if way == 0 else (z + hop <= nhead - 1)

            @pl.when(there)
            def _():
                grad_product(z - hop if way == 0 else z + hop)

    def rounded_grad(h):
        da = acc[:, lanes(h)].astype(BF16)
        return jnp.where(live, da.astype(F32), 0.0)

    def recall_back(h, da):
        dnum = da * ginv_ref[:, lanes(h)]
        dden = -jnp.sum(dnum * recalled_ref[:, lanes(h)].astype(F32), axis=1, keepdims=True)
        high = dden.astype(BF16).astype(F32)
        lane = lax.broadcasted_iota(jnp.int32, (seg, EXT), 1)
        tail = jnp.where(lane == 0, high, jnp.where(lane == 1, dden - high, 0.0))
        return jnp.concatenate([dnum.astype(BF16), tail.astype(BF16)], axis=1)

    @over_heads
    def _(h):
        ext = recall_back(h, rounded_grad(h))
        out = dot(ext, lifted_ref[:, lanes(h)], 0, 0)
        gm_own[h, :hd] = out[:hd].astype(BF16)
        norm = out[hd:hd + 1] + out[hd + 1:hd + 2]
        row = lax.broadcasted_iota(jnp.int32, (EXT, hd), 0)
        gm_own[h, hd:] = jnp.where(row == 0, norm, 0.0).astype(BF16)

    for d in range(1, span):
        gm_copy(d).start()

    @over_heads
    def _(h):
        da = rounded_grad(h)
        ext = recall_back(h, da)
        dlifted = dot(ext, mem_ref[h], 1, 0)
        do = ((1.0 - gate_of(h)) * da).astype(BF16)
        p = probs[h]
        dv_ref[:, lanes(h)] = dot(p, do, 0, 0)
        dp = dot(do, v_ref[:, lanes(h)], 1, 1)
        p32 = p.astype(F32)
        weighted = p32 * dp
        ds = (weighted - p32 * jnp.sum(weighted, axis=1, keepdims=True)).astype(BF16)
        dk_ref[:, lanes(h)] = dot(ds, q_ref[:, lanes(h)], 0, 0) * scale
        dq = dot(ds, k_ref[:, lanes(h)], 1, 0) * scale
        dq_ref[:, lanes(h)] = (
            dq + dlifted * lift_slope(q_ref[:, lanes(h)].astype(F32))
        ).astype(BF16)

    for d in range(1, span):
        gm_copy(d).wait_recv()

    @over_heads
    def _(h):
        total = total_state(gm_in, False, h).astype(BF16)
        k32 = k_ref[:, lanes(h)].astype(F32)
        dlifted = dot(with_ones(v_ref[:, lanes(h)]), total, 1, 0)
        slope = jnp.where(live, lift_slope(k32), 0.0)
        gk_ref[:, lanes(h)] = (dk_ref[:, lanes(h)] + dlifted * slope).astype(BF16)
        lifted = jnp.where(live, lift(k32), 0.0).astype(BF16)
        gv_ref[:, lanes(h)] = (
            dv_ref[:, lanes(h)] + dot(lifted, total[:hd], 1, 1)
        ).astype(BF16)

    for step in range(1, nhead):
        other = (z + step) % nhead
        for sub in range(per):
            remote(
                terms.at[sub], parts.at[other, sub], p_send.at[sub], p_recv.at[other, sub], me,
                other,
            ).wait_recv()
    for sub in range(per):
        total = terms[z * per + sub].astype(F32)
        for step in range(1, nhead):
            total = total + parts[(z + step) % nhead, sub].astype(F32)
        mixed_ref[:, sub * wcols:(sub + 1) * wcols] = total.astype(BF16)

    for step in range(1, nhead):
        for sub in range(per):
            p_copy(((z + step) % nhead) * per + sub).wait_send()
    for d in range(1, span):
        kv_copy(d).wait_send()
        gm_copy(d).wait_send()
    for delta in range(chips):
        w_to_partner(delta).wait_send()
        if delta > 0:
            w_to_chip(delta).wait_send()
    for way in range(2):
        for hop in range(nhead - 1):

            @pl.when(u_sends(way, hop))
            def _():
                u_copy(way, hop).wait_send()


def per_device(q, k, v, upstream, out_weight, gate_logit, document_ids, valid_lengths):
    heads = gate_logit.shape[0]
    seg, width = q.shape
    hd = width // heads
    nseq, nhead = lax.axis_size("seq"), lax.axis_size("head")
    wcols = out_weight.shape[1]
    per = nseq // nhead
    span = nseq // 2
    state = (heads, hd + EXT, hd)
    dma = pltpu.SemaphoreType.DMA
    smem = pl.BlockSpec(memory_space=pltpu.SMEM)
    vmem = pl.BlockSpec(memory_space=pltpu.VMEM)
    return pl.pallas_call(
        functools.partial(kernel, nseq, nhead, heads),
        out_shape=[jax.ShapeDtypeStruct((seg, width), BF16)] * 4,
        in_specs=[smem] * 3 + [vmem] * 5,
        out_specs=[vmem] * 4,
        scratch_shapes=[
            pltpu.VMEM((nseq, width, wcols), BF16),
            pltpu.VMEM((nhead, seg, wcols * per), BF16),
            pltpu.VMEM((nseq, seg, wcols), BF16),
            pltpu.VMEM((nhead, per, seg, wcols), BF16),
            pltpu.VMEM((heads, seg, seg), BF16),
            pltpu.VMEM((seg, width), F32),
            pltpu.VMEM((seg, width), BF16),
            pltpu.VMEM((seg, width), BF16),
            pltpu.VMEM((seg, width), F32),
            pltpu.VMEM((seg, width), F32),
            pltpu.VMEM((seg, width), F32),
            pltpu.VMEM((seg, width), BF16),
            pltpu.VMEM((seg, width), BF16),
            pltpu.VMEM(state, BF16),
            pltpu.VMEM(state, BF16),
            pltpu.VMEM((span - 1,) + state, BF16),
            pltpu.VMEM(state, BF16),
            pltpu.VMEM((span - 1,) + state, BF16),
            dma((span,)), dma((span,)), dma((nseq,)),
            dma((2, nhead)), dma((nhead,)),
            dma((span - 1,)), dma((span - 1,)), dma((span - 1,)), dma((span - 1,)),
            dma((nseq,)), dma((nhead, per)), dma((2,)),
        ],
        compiler_params=pltpu.CompilerParams(
            collective_id=0, has_side_effects=True, vmem_limit_bytes=60 * 1024 * 1024
        ),
        cost_estimate=pl.CostEstimate(
            flops=4 * seg * width * wcols * nseq, bytes_accessed=18 * seg * width,
            transcendentals=0,
        ),
        name="layer",
    )(valid_lengths, document_ids, gate_logit, q, k, v, upstream, out_weight)


def solution(mesh):
    spec = P("seq", "head")
    return jax.shard_map(
        per_device,
        mesh=mesh,
        in_specs=(spec, spec, spec, spec, P("head", "seq"), P("head"), P(), P()),
        out_specs=(spec, spec, spec, spec),
        check_vma=False,
    )
```

```python
import functools

import jax
import jax.numpy as jnp
from jax import lax
from jax.experimental import pallas as pl
from jax.experimental.pallas import tpu as pltpu
from jax.sharding import PartitionSpec as P

F32 = jnp.float32
BF16 = jnp.bfloat16
EXT = 16
LAG = 2
MESH = pl.DeviceIdType.MESH


def lift(x):
    return jnp.where(x > 0, x + 1.0, jnp.exp(jnp.minimum(x, 0.0)))


def lift_slope(x):
    return jnp.where(x > 0, 1.0, jnp.exp(jnp.minimum(x, 0.0)))


def dot(a, b, ca, cb):
    return lax.dot_general(a, b, (((ca,), (cb,)), ((), ())), preferred_element_type=F32)


def row_mask(rows, valid, first=0):
    return lax.broadcasted_iota(jnp.int32, (rows, 1), 0) + first < valid


def with_ones(v):
    return jnp.concatenate([v, jnp.ones((v.shape[0], EXT), v.dtype)], axis=1)


def kernel(
    nseq, nhead, heads,
    valid_ref, doc_ref, gate_ref, q_ref, k_ref, v_ref, u_ref, w_ref,
    mixed_ref, dq_ref, gk_ref, gv_ref,
    wall, uall, right_ref, left_ref, probs, acc, lifted_ref, recalled_ref, ginv_ref,
    dk_ref, dv_ref, attn_ref, da_ref, mem_ref, kv_own, kv_in, gm_own, gm_in,
    w_send, w_pass, w_recv, u_send, u_recv, kv_send, kv_recv, gm_send, gm_recv,
    hop_send, hop_recv, own_sem,
):
    seg, width = q_ref.shape
    hd = width // heads
    half = seg // 2
    span = nseq // 2
    chips = nseq // 2
    per = nseq // nhead
    wcols = w_ref.shape[1]
    scale = hd ** -0.5
    me = lax.axis_index("seq")
    z = lax.axis_index("head")
    chip, core = me // 2, me % 2
    partner = chip * 2 + 1 - core
    has_left, has_right = z > 0, z < nhead - 1

    barrier = pltpu.get_barrier_semaphore()
    for d in range(1, nseq):
        pl.semaphore_signal(
            barrier, inc=1, device_id=((me + d) % nseq, z), device_id_type=MESH
        )

    for d in range(1, nhead):
        pl.semaphore_signal(
            barrier, inc=1, device_id=(me, (z + d) % nhead), device_id_type=MESH
        )
    pl.semaphore_wait(barrier, nseq + nhead - 2)

    def remote(src, dst, send, recv, seq, head):
        return pltpu.make_async_remote_copy(
            src_ref=src, dst_ref=dst, send_sem=send, recv_sem=recv,
            device_id=(seq, head), device_id_type=MESH,
        )

    def u_copy(way, hop):
        block = z - hop if way == 0 else z + hop
        to = z + 1 if way == 0 else z - 1
        src = u_ref if hop == 0 else uall.at[block]
        return remote(src, uall.at[block], u_send.at[way, hop], u_recv.at[block], me, to)

    def u_sends(way, hop):
        if way == 0:
            return has_right & (z >= hop)
        return has_left & (z + hop <= nhead - 1)

    def u_wait(block):
        remote(u_ref, uall.at[block], u_send.at[0, 0], u_recv.at[block], me, z).wait_recv()

    def u_arrived(hop):
        for way in range(2):
            block = z - hop if way == 0 else z + hop
            there = (z >= hop) if way == 0 else (z + hop <= nhead - 1)

            @pl.when(there)
            def _():
                u_wait(block)

            if hop < nhead - 1:

                @pl.when(u_sends(way, hop))
                def _():
                    u_copy(way, hop).start()

    for way in range(2):

        @pl.when(u_sends(way, 0))
        def _():
            u_copy(way, 0).start()

    def w_to_partner(delta):
        block = ((chip - delta + chips) % chips) * 2 + core
        src = w_ref if delta == 0 else wall.at[block]
        return remote(src, wall.at[block], w_pass.at[delta], w_recv.at[block], partner, z)

    def w_to_chip(delta):
        to = ((chip + delta) % chips) * 2 + core
        return remote(w_ref, wall.at[me], w_send.at[delta], w_recv.at[me], to, z)

    def w_wait(block):
        remote(w_ref, wall.at[block], w_pass.at[0], w_recv.at[block], partner, z).wait_recv()

    w_to_partner(0).start()
    own_w = pltpu.make_async_copy(w_ref, wall.at[me], own_sem.at[0])
    own_w.start()
    own_u = pltpu.make_async_copy(u_ref, uall.at[z], own_sem.at[1])
    own_u.start()

    valid = valid_ref[me]
    live = row_mask(seg, valid)

    def lanes(h):
        return pl.ds(pl.multiple_of(h * hd, hd), hd)

    def gate_of(h):
        return 1.0 / (1.0 + jnp.exp(jnp.full((1, hd), -gate_ref[h], F32)))

    def over_heads(body):
        def step(h, carry):
            body(h)
            return carry

        lax.fori_loop(0, heads, step, 0)

    @over_heads
    def _(h):
        lifted = jnp.where(live, lift(k_ref[:, lanes(h)].astype(F32)), 0.0).astype(BF16)
        kv_own[h] = dot(with_ones(v_ref[:, lanes(h)]), lifted, 0, 0).astype(BF16)

    def kv_copy(d):
        return remote(
            kv_own, kv_in.at[d - 1], kv_send.at[d - 1], kv_recv.at[d - 1], (me + d) % nseq, z
        )

    def gm_copy(d):
        return remote(
            gm_own, gm_in.at[d - 1], gm_send.at[d - 1], gm_recv.at[d - 1],
            (me - d + nseq) % nseq, z,
        )

    for d in range(1, span):

        @pl.when(me + d < nseq)
        def _():
            kv_copy(d).start()

    for delta in range(1, chips):
        w_to_chip(delta).start()

    @over_heads
    def _(h):
        keep = 1.0 - gate_of(h)
        probs[h, :half, half:] = jnp.zeros((half, seg - half), BF16)
        for first, count in ((0, half), (half, seg)):
            rows = slice(first, first + half)
            s = dot(q_ref[rows, lanes(h)], k_ref[:count, lanes(h)], 1, 1) * scale
            r = lax.broadcasted_iota(jnp.int32, (half, count), 0) + first
            c = lax.broadcasted_iota(jnp.int32, (half, count), 1)
            s = jnp.where((c <= r) & (c < valid), s, -1e30)
            e = jnp.exp(s - jnp.max(s, axis=1, keepdims=True))
            p = (e * (1.0 / jnp.sum(e, axis=1, keepdims=True))).astype(BF16)
            probs[h, rows, :count] = p
            acc[rows, lanes(h)] = keep * dot(p, v_ref[:count, lanes(h)], 1, 0)

    def weight_of(d, earlier):
        other = me - d if earlier else me + d
        inside = (other >= 0) if earlier else (other < nseq)
        index = (other + nseq) % nseq
        return (inside & (doc_ref[index] == doc_ref[me])).astype(F32)

    for d in range(1, span):

        @pl.when(me >= d)
        def _():
            kv_copy(d).wait_recv()

        @pl.when(me < d)
        def _():
            kv_in[d - 1] = jnp.zeros(kv_in.shape[1:], BF16)

    def total_state(slots, earlier, h):
        total = jnp.zeros((hd + EXT, hd), F32)
        for d in range(1, span):
            total = total + weight_of(d, earlier) * slots[d - 1, h].astype(F32)
        return total

    @over_heads
    def _(h):
        gate = gate_of(h)
        mem = total_state(kv_in, True, h).astype(BF16)
        mem_ref[h] = mem
        lifted = lift(q_ref[:, lanes(h)].astype(F32)).astype(BF16)
        lifted_ref[:, lanes(h)] = lifted
        recall = dot(lifted, mem, 1, 1)
        inv = 1.0 / (1.0 + recall[:, hd:hd + 1])
        recalled = recall[:, :hd] * inv
        recalled_ref[:, lanes(h)] = recalled.astype(BF16)
        ginv_ref[:, lanes(h)] = jnp.where(live, gate * inv, 0.0)
        attn = gate * recalled + acc[:, lanes(h)]
        attn_ref[:, lanes(h)] = jnp.where(live, attn, 0.0).astype(BF16)

    def block_at(i):
        delta, kind = i // 2, i % 2
        return ((chip - delta + chips) % chips) * 2 + (core + kind) % 2

    def hop_copy(way, block):
        slots = right_ref if way == 0 else left_ref
        to = z + 1 if way == 0 else z - 1
        return remote(
            slots.at[block], slots.at[block], hop_send.at[way, block], hop_recv.at[way, block],
            me, to,
        )

    def project(block):
        return dot(attn_ref[...], wall[block], 1, 0)

    def tick(now):
        for way in range(2):
            slots = right_ref if way == 0 else left_ref
            place = z if way == 0 else nhead - 1 - z
            i = now - place * LAG

            @pl.when((i >= 0) & (i < nseq))
            def _():
                block = block_at(i)
                owner = block // per

                @pl.when(owner > z if way == 0 else owner < z)
                def _():
                    @pl.when(place > 0)
                    def _():
                        hop_copy(way, block).wait_recv()
                        slots[block] = (project(block) + slots[block].astype(F32)).astype(BF16)

                    @pl.when(place == 0)
                    def _():
                        slots[block] = project(block).astype(BF16)

                    hop_copy(way, block).start()

    def ticks(first, last):
        def step(now, carry):
            tick(now)
            return carry

        lax.fori_loop(first, last, step, 0)

    own_w.wait()
    tick(0)
    w_wait(partner)
    tick(1)
    for delta in range(1, chips):
        base = ((chip - delta + chips) % chips) * 2
        w_wait(base + core)
        w_to_partner(delta).start()
        if delta < nhead - 1:
            u_arrived(delta)
        tick(2 * delta)
        w_wait(base + 1 - core)
        tick(2 * delta + 1)

    def grad_product(block):
        for sub in range(per):
            acc[...] += dot(
                uall[block, :, sub * wcols:(sub + 1) * wcols], wall[block * per + sub], 1, 1
            )

    own_u.wait()
    acc[...] = jnp.zeros_like(acc)
    grad_product(z)
    for hop in range(1, nhead):
        if hop == nhead - 1:
            ticks(nseq, nseq + LAG)
        if hop >= min(chips, nhead - 1):
            u_arrived(hop)
        for way in range(2):
            there = (z >= hop) if way == 0 else (z + hop <= nhead - 1)

            @pl.when(there)
            def _():
                grad_product(z - hop if way == 0 else z + hop)

    def rounded_grad(h):
        da = acc[:, lanes(h)].astype(BF16)
        return jnp.where(live, da.astype(F32), 0.0)

    def recall_back(h, da):
        dnum = da * ginv_ref[:, lanes(h)]
        dden = -jnp.sum(dnum * recalled_ref[:, lanes(h)].astype(F32), axis=1, keepdims=True)
        high = dden.astype(BF16).astype(F32)
        lane = lax.broadcasted_iota(jnp.int32, (seg, EXT), 1)
        tail = jnp.where(lane == 0, high, jnp.where(lane == 1, dden - high, 0.0))
        return jnp.concatenate([dnum.astype(BF16), tail.astype(BF16)], axis=1)

    @over_heads
    def _(h):
        ext = recall_back(h, rounded_grad(h))
        out = dot(ext, lifted_ref[:, lanes(h)], 0, 0)
        gm_own[h, :hd] = out[:hd].astype(BF16)
        norm = out[hd:hd + 1] + out[hd + 1:hd + 2]
        row = lax.broadcasted_iota(jnp.int32, (EXT, hd), 0)
        gm_own[h, hd:] = jnp.where(row == 0, norm, 0.0).astype(BF16)

    for d in range(1, span):

        @pl.when(me >= d)
        def _():
            gm_copy(d).start()

    ticks(nseq + LAG, nseq + (nhead - 2) * LAG)

    @over_heads
    def _(h):
        da = rounded_grad(h)
        ext = recall_back(h, da)
        dlifted = dot(ext, mem_ref[h], 1, 0)
        do = ((1.0 - gate_of(h)) * da).astype(BF16)
        p = probs[h]
        dv_ref[:, lanes(h)] = dot(p, do, 0, 0)
        dp = dot(do, v_ref[:, lanes(h)], 1, 1)
        p32 = p.astype(F32)
        weighted = p32 * dp
        ds = (weighted - p32 * jnp.sum(weighted, axis=1, keepdims=True)).astype(BF16)
        dk_ref[:, lanes(h)] = dot(ds, q_ref[:, lanes(h)], 0, 0) * scale
        dq = dot(ds, k_ref[:, lanes(h)], 1, 0) * scale
        dq_ref[:, lanes(h)] = (
            dq + dlifted * lift_slope(q_ref[:, lanes(h)].astype(F32))
        ).astype(BF16)

    for d in range(1, span):

        @pl.when(me + d < nseq)
        def _():
            gm_copy(d).wait_recv()

        @pl.when(me + d >= nseq)
        def _():
            gm_in[d - 1] = jnp.zeros(gm_in.shape[1:], BF16)

    @over_heads
    def _(h):
        total = total_state(gm_in, False, h).astype(BF16)
        k32 = k_ref[:, lanes(h)].astype(F32)
        dlifted = dot(with_ones(v_ref[:, lanes(h)]), total, 1, 0)
        slope = jnp.where(live, lift_slope(k32), 0.0)
        gk_ref[:, lanes(h)] = (dk_ref[:, lanes(h)] + dlifted * slope).astype(BF16)
        lifted = jnp.where(live, lift(k32), 0.0).astype(BF16)
        gv_ref[:, lanes(h)] = (
            dv_ref[:, lanes(h)] + dot(lifted, total[:hd], 1, 1)
        ).astype(BF16)

    for sub in range(per):
        cols = slice(sub * wcols, (sub + 1) * wcols)
        block = z * per + sub
        acc[:, cols] = project(block)
        for way in range(2):
            slots = right_ref if way == 0 else left_ref

            @pl.when(has_left if way == 0 else has_right)
            def _():
                hop_copy(way, block).wait_recv()
                acc[:, cols] += slots[block].astype(F32)

        mixed_ref[:, cols] = acc[:, cols].astype(BF16)

    def sent(block, carry):
        for way in range(2):

            @pl.when(block // per > z if way == 0 else block // per < z)
            def _():
                hop_copy(way, block).wait_send()

        return carry

    lax.fori_loop(0, nseq, sent, 0)
    for d in range(1, span):

        @pl.when(me + d < nseq)
        def _():
            kv_copy(d).wait_send()

        @pl.when(me >= d)
        def _():
            gm_copy(d).wait_send()

    for delta in range(chips):
        w_to_partner(delta).wait_send()
        if delta > 0:
            w_to_chip(delta).wait_send()
    for way in range(2):
        for hop in range(nhead - 1):

            @pl.when(u_sends(way, hop))
            def _():
                u_copy(way, hop).wait_send()


def per_device(q, k, v, upstream, out_weight, gate_logit, document_ids, valid_lengths):
    heads = gate_logit.shape[0]
    seg, width = q.shape
    hd = width // heads
    nseq, nhead = lax.axis_size("seq"), lax.axis_size("head")
    wcols = out_weight.shape[1]
    per = nseq // nhead
    span = nseq // 2
    state = (heads, hd + EXT, hd)
    dma = pltpu.SemaphoreType.DMA
    smem = pl.BlockSpec(memory_space=pltpu.SMEM)
    vmem = pl.BlockSpec(memory_space=pltpu.VMEM)
    return pl.pallas_call(
        functools.partial(kernel, nseq, nhead, heads),
        out_shape=[jax.ShapeDtypeStruct((seg, width), BF16)] * 4,
        in_specs=[smem] * 3 + [vmem] * 5,
        out_specs=[vmem] * 4,
        scratch_shapes=[
            pltpu.VMEM((nseq, width, wcols), BF16),
            pltpu.VMEM((nhead, seg, wcols * per), BF16),
            pltpu.VMEM((nseq, seg, wcols), BF16),
            pltpu.VMEM((nseq, seg, wcols), BF16),
            pltpu.VMEM((heads, seg, seg), BF16),
            pltpu.VMEM((seg, width), F32),
            pltpu.VMEM((seg, width), BF16),
            pltpu.VMEM((seg, width), BF16),
            pltpu.VMEM((seg, width), F32),
            pltpu.VMEM((seg, width), F32),
            pltpu.VMEM((seg, width), F32),
            pltpu.VMEM((seg, width), BF16),
            pltpu.VMEM((seg, width), BF16),
            pltpu.VMEM(state, BF16),
            pltpu.VMEM(state, BF16),
            pltpu.VMEM((span - 1,) + state, BF16),
            pltpu.VMEM(state, BF16),
            pltpu.VMEM((span - 1,) + state, BF16),
            dma((span,)), dma((span,)), dma((nseq,)),
            dma((2, nhead)), dma((nhead,)),
            dma((span - 1,)), dma((span - 1,)), dma((span - 1,)), dma((span - 1,)),
            dma((2, nseq)), dma((2, nseq)), dma((2,)),
        ],
        compiler_params=pltpu.CompilerParams(
            collective_id=0, has_side_effects=True, vmem_limit_bytes=60 * 1024 * 1024
        ),
        cost_estimate=pl.CostEstimate(
            flops=4 * seg * width * wcols * nseq, bytes_accessed=18 * seg * width,
            transcendentals=0,
        ),
        name="layer",
    )(valid_lengths, document_ids, gate_logit, q, k, v, upstream, out_weight)


def solution(mesh):
    spec = P("seq", "head")
    return jax.shard_map(
        per_device,
        mesh=mesh,
        in_specs=(spec, spec, spec, spec, P("head", "seq"), P("head"), P(), P()),
        out_specs=(spec, spec, spec, spec),
        check_vma=False,
    )
```

```python
import functools

import jax
import jax.numpy as jnp
from jax import lax
from jax.experimental import pallas as pl
from jax.experimental.pallas import tpu as pltpu
from jax.sharding import PartitionSpec as P

F32 = jnp.float32
BF16 = jnp.bfloat16
EXT = 16
LAG = 2
MESH = pl.DeviceIdType.MESH


def lift(x):
    return jnp.where(x > 0, x + 1.0, jnp.exp(jnp.minimum(x, 0.0)))


def lift_slope(x):
    return jnp.where(x > 0, 1.0, jnp.exp(jnp.minimum(x, 0.0)))


def dot(a, b, ca, cb):
    return lax.dot_general(a, b, (((ca,), (cb,)), ((), ())), preferred_element_type=F32)


def row_mask(rows, valid, first=0):
    return lax.broadcasted_iota(jnp.int32, (rows, 1), 0) + first < valid


def with_ones(v):
    return jnp.concatenate([v, jnp.ones((v.shape[0], EXT), v.dtype)], axis=1)


def kernel(
    nseq, nhead, heads,
    valid_ref, doc_ref, gate_ref, q_ref, k_ref, v_ref, u_ref, w_ref,
    mixed_ref, dq_ref, gk_ref, gv_ref,
    wall, uall, right_ref, left_ref, probs, acc, lifted_ref, recalled_ref, ginv_ref,
    dk_ref, dv_ref, attn_ref, da_ref, mem_ref, kv_own, kv_in, gm_own, gm_in,
    w_send, w_pass, w_recv, u_send, u_recv, kv_send, kv_recv, gm_send, gm_recv,
    hop_send, hop_recv, own_sem,
):
    seg, width = q_ref.shape
    hd = width // heads
    half = seg // 2
    span = nseq // 2
    chips = nseq // 2
    per = nseq // nhead
    wcols = w_ref.shape[1]
    scale = hd ** -0.5
    me = lax.axis_index("seq")
    z = lax.axis_index("head")
    chip, core = me // 2, me % 2
    partner = chip * 2 + 1 - core
    has_left, has_right = z > 0, z < nhead - 1

    barrier = pltpu.get_barrier_semaphore()
    for d in range(1, nseq):
        pl.semaphore_signal(
            barrier, inc=1, device_id=((me + d) % nseq, z), device_id_type=MESH
        )

    for d in range(1, nhead):
        pl.semaphore_signal(
            barrier, inc=1, device_id=(me, (z + d) % nhead), device_id_type=MESH
        )
    pl.semaphore_wait(barrier, nseq + nhead - 2)

    def remote(src, dst, send, recv, seq, head):
        return pltpu.make_async_remote_copy(
            src_ref=src, dst_ref=dst, send_sem=send, recv_sem=recv,
            device_id=(seq, head), device_id_type=MESH,
        )

    def u_copy(way, hop):
        block = z - hop if way == 0 else z + hop
        to = z + 1 if way == 0 else z - 1
        src = u_ref if hop == 0 else uall.at[block]
        return remote(src, uall.at[block], u_send.at[way, hop], u_recv.at[block], me, to)

    def u_sends(way, hop):
        if way == 0:
            return has_right & (z >= hop)
        return has_left & (z + hop <= nhead - 1)

    def u_wait(block):
        remote(u_ref, uall.at[block], u_send.at[0, 0], u_recv.at[block], me, z).wait_recv()

    def u_arrived(hop):
        for way in range(2):
            block = z - hop if way == 0 else z + hop
            there = (z >= hop) if way == 0 else (z + hop <= nhead - 1)

            @pl.when(there)
            def _():
                u_wait(block)

            if hop < nhead - 1:

                @pl.when(u_sends(way, hop))
                def _():
                    u_copy(way, hop).start()

    for way in range(2):

        @pl.when(u_sends(way, 0))
        def _():
            u_copy(way, 0).start()

    def w_to_partner(delta):
        block = ((chip - delta + chips) % chips) * 2 + core
        src = w_ref if delta == 0 else wall.at[block]
        return remote(src, wall.at[block], w_pass.at[delta], w_recv.at[block], partner, z)

    def w_to_chip(delta):
        to = ((chip + delta) % chips) * 2 + core
        return remote(w_ref, wall.at[me], w_send.at[delta], w_recv.at[me], to, z)

    def w_wait(block):
        remote(w_ref, wall.at[block], w_pass.at[0], w_recv.at[block], partner, z).wait_recv()

    w_to_partner(0).start()
    own_w = pltpu.make_async_copy(w_ref, wall.at[me], own_sem.at[0])
    own_w.start()
    own_u = pltpu.make_async_copy(u_ref, uall.at[z], own_sem.at[1])
    own_u.start()

    valid = valid_ref[me]
    live = row_mask(seg, valid)

    def lanes(h):
        return pl.ds(pl.multiple_of(h * hd, hd), hd)

    def gate_of(h):
        return 1.0 / (1.0 + jnp.exp(jnp.full((1, hd), -gate_ref[h], F32)))

    def over_heads(body):
        def step(h, carry):
            body(h)
            return carry

        lax.fori_loop(0, heads, step, 0)

    @over_heads
    def _(h):
        lifted = jnp.where(live, lift(k_ref[:, lanes(h)].astype(F32)), 0.0).astype(BF16)
        kv_own[h] = dot(with_ones(v_ref[:, lanes(h)]), lifted, 0, 0).astype(BF16)

    def kv_copy(d):
        return remote(
            kv_own, kv_in.at[d - 1], kv_send.at[d - 1], kv_recv.at[d - 1], (me + d) % nseq, z
        )

    def gm_copy(d):
        return remote(
            gm_own, gm_in.at[d - 1], gm_send.at[d - 1], gm_recv.at[d - 1],
            (me - d + nseq) % nseq, z,
        )

    for d in range(1, span):

        @pl.when(me + d < nseq)
        def _():
            kv_copy(d).start()

    for delta in range(1, chips):
        w_to_chip(delta).start()

    @over_heads
    def _(h):
        keep = 1.0 - gate_of(h)
        probs[h, :half, half:] = jnp.zeros((half, seg - half), BF16)
        for first, count in ((0, half), (half, seg)):
            rows = slice(first, first + half)
            s = dot(q_ref[rows, lanes(h)], k_ref[:count, lanes(h)], 1, 1) * scale
            r = lax.broadcasted_iota(jnp.int32, (half, count), 0) + first
            c = lax.broadcasted_iota(jnp.int32, (half, count), 1)
            s = jnp.where((c <= r) & (c < valid), s, -1e30)
            e = jnp.exp(s - jnp.max(s, axis=1, keepdims=True))
            p = (e * (1.0 / jnp.sum(e, axis=1, keepdims=True))).astype(BF16)
            probs[h, rows, :count] = p
            acc[rows, lanes(h)] = keep * dot(p, v_ref[:count, lanes(h)], 1, 0)

    def weight_of(d, earlier):
        other = me - d if earlier else me + d
        inside = (other >= 0) if earlier else (other < nseq)
        index = (other + nseq) % nseq
        return (inside & (doc_ref[index] == doc_ref[me])).astype(F32)

    for d in range(1, span):

        @pl.when(me >= d)
        def _():
            kv_copy(d).wait_recv()

        @pl.when(me < d)
        def _():
            kv_in[d - 1] = jnp.zeros(kv_in.shape[1:], BF16)

    def total_state(slots, earlier, h):
        total = jnp.zeros((hd + EXT, hd), F32)
        for d in range(1, span):
            total = total + weight_of(d, earlier) * slots[d - 1, h].astype(F32)
        return total

    @over_heads
    def _(h):
        gate = gate_of(h)
        mem = total_state(kv_in, True, h).astype(BF16)
        mem_ref[h] = mem
        lifted = lift(q_ref[:, lanes(h)].astype(F32)).astype(BF16)
        lifted_ref[:, lanes(h)] = lifted
        recall = dot(lifted, mem, 1, 1)
        inv = 1.0 / (1.0 + recall[:, hd:hd + 1])
        recalled = recall[:, :hd] * inv
        recalled_ref[:, lanes(h)] = recalled.astype(BF16)
        ginv_ref[:, lanes(h)] = jnp.where(live, gate * inv, 0.0)
        attn = gate * recalled + acc[:, lanes(h)]
        attn_ref[:, lanes(h)] = jnp.where(live, attn, 0.0).astype(BF16)

    def block_at(i):
        delta, kind = i // 2, i % 2
        return ((chip - delta + chips) % chips) * 2 + (core + kind) % 2

    def hop_copy(way, block):
        slots = right_ref if way == 0 else left_ref
        to = z + 1 if way == 0 else z - 1
        return remote(
            slots.at[block], slots.at[block], hop_send.at[way, block], hop_recv.at[way, block],
            me, to,
        )

    def project(block):
        return dot(attn_ref[...], wall[block], 1, 0)

    def tick(now):
        for way in range(2):
            slots = right_ref if way == 0 else left_ref
            place = z if way == 0 else nhead - 1 - z
            i = now - place * LAG

            @pl.when((i >= 0) & (i < nseq))
            def _():
                block = block_at(i)
                owner = block // per

                @pl.when(owner > z if way == 0 else owner < z)
                def _():
                    @pl.when(place > 0)
                    def _():
                        hop_copy(way, block).wait_recv()
                        slots[block] = (project(block) + slots[block].astype(F32)).astype(BF16)

                    @pl.when(place == 0)
                    def _():
                        slots[block] = project(block).astype(BF16)

                    hop_copy(way, block).start()

    def ticks(first, last):
        def step(now, carry):
            tick(now)
            return carry

        lax.fori_loop(first, last, step, 0)

    if nhead > 2:
        u_arrived(1)
    own_w.wait()
    tick(0)
    w_wait(partner)
    tick(1)
    for delta in range(1, chips):
        base = ((chip - delta + chips) % chips) * 2
        w_wait(base + core)
        w_to_partner(delta).start()
        tick(2 * delta)
        w_wait(base + 1 - core)
        tick(2 * delta + 1)
        if delta + 1 < nhead - 1:
            u_arrived(delta + 1)

    def grad_product(block):
        for sub in range(per):
            acc[...] += dot(
                uall[block, :, sub * wcols:(sub + 1) * wcols], wall[block * per + sub], 1, 1
            )

    own_u.wait()
    acc[...] = jnp.zeros_like(acc)
    grad_product(z)
    for hop in range(1, nhead):
        if hop == nhead - 1:
            ticks(nseq, nseq + LAG)
        if hop > chips or hop == nhead - 1:
            u_arrived(hop)
        for way in range(2):
            there = (z >= hop) if way == 0 else (z + hop <= nhead - 1)

            @pl.when(there)
            def _():
                grad_product(z - hop if way == 0 else z + hop)

    def rounded_grad(h):
        da = acc[:, lanes(h)].astype(BF16)
        return jnp.where(live, da.astype(F32), 0.0)

    def recall_back(h, da):
        dnum = da * ginv_ref[:, lanes(h)]
        dden = -jnp.sum(dnum * recalled_ref[:, lanes(h)].astype(F32), axis=1, keepdims=True)
        high = dden.astype(BF16).astype(F32)
        lane = lax.broadcasted_iota(jnp.int32, (seg, EXT), 1)
        tail = jnp.where(lane == 0, high, jnp.where(lane == 1, dden - high, 0.0))
        return jnp.concatenate([dnum.astype(BF16), tail.astype(BF16)], axis=1)

    @over_heads
    def _(h):
        ext = recall_back(h, rounded_grad(h))
        out = dot(ext, lifted_ref[:, lanes(h)], 0, 0)
        gm_own[h, :hd] = out[:hd].astype(BF16)
        norm = out[hd:hd + 1] + out[hd + 1:hd + 2]
        row = lax.broadcasted_iota(jnp.int32, (EXT, hd), 0)
        gm_own[h, hd:] = jnp.where(row == 0, norm, 0.0).astype(BF16)

    for d in range(1, span):

        @pl.when(me >= d)
        def _():
            gm_copy(d).start()

    ticks(nseq + LAG, nseq + (nhead - 2) * LAG)

    @over_heads
    def _(h):
        da = rounded_grad(h)
        ext = recall_back(h, da)
        dlifted = dot(ext, mem_ref[h], 1, 0)
        do = ((1.0 - gate_of(h)) * da).astype(BF16)
        p = probs[h]
        dv_ref[:, lanes(h)] = dot(p, do, 0, 0)
        dp = dot(do, v_ref[:, lanes(h)], 1, 1)
        p32 = p.astype(F32)
        weighted = p32 * dp
        ds = (weighted - p32 * jnp.sum(weighted, axis=1, keepdims=True)).astype(BF16)
        dk_ref[:, lanes(h)] = dot(ds, q_ref[:, lanes(h)], 0, 0) * scale
        dq = dot(ds, k_ref[:, lanes(h)], 1, 0) * scale
        dq_ref[:, lanes(h)] = (
            dq + dlifted * lift_slope(q_ref[:, lanes(h)].astype(F32))
        ).astype(BF16)

    for d in range(1, span):

        @pl.when(me + d < nseq)
        def _():
            gm_copy(d).wait_recv()

        @pl.when(me + d >= nseq)
        def _():
            gm_in[d - 1] = jnp.zeros(gm_in.shape[1:], BF16)

    @over_heads
    def _(h):
        total = total_state(gm_in, False, h).astype(BF16)
        k32 = k_ref[:, lanes(h)].astype(F32)
        dlifted = dot(with_ones(v_ref[:, lanes(h)]), total, 1, 0)
        slope = jnp.where(live, lift_slope(k32), 0.0)
        gk_ref[:, lanes(h)] = (dk_ref[:, lanes(h)] + dlifted * slope).astype(BF16)
        lifted = jnp.where(live, lift(k32), 0.0).astype(BF16)
        gv_ref[:, lanes(h)] = (
            dv_ref[:, lanes(h)] + dot(lifted, total[:hd], 1, 1)
        ).astype(BF16)

    for sub in range(per):
        cols = slice(sub * wcols, (sub + 1) * wcols)
        block = z * per + sub
        acc[:, cols] = project(block)
        for way in range(2):
            slots = right_ref if way == 0 else left_ref

            @pl.when(has_left if way == 0 else has_right)
            def _():
                hop_copy(way, block).wait_recv()
                acc[:, cols] += slots[block].astype(F32)

        mixed_ref[:, cols] = acc[:, cols].astype(BF16)

    def sent(block, carry):
        for way in range(2):

            @pl.when(block // per > z if way == 0 else block // per < z)
            def _():
                hop_copy(way, block).wait_send()

        return carry

    lax.fori_loop(0, nseq, sent, 0)
    for d in range(1, span):

        @pl.when(me + d < nseq)
        def _():
            kv_copy(d).wait_send()

        @pl.when(me >= d)
        def _():
            gm_copy(d).wait_send()

    for delta in range(chips):
        w_to_partner(delta).wait_send()
        if delta > 0:
            w_to_chip(delta).wait_send()
    for way in range(2):
        for hop in range(nhead - 1):

            @pl.when(u_sends(way, hop))
            def _():
                u_copy(way, hop).wait_send()


def per_device(q, k, v, upstream, out_weight, gate_logit, document_ids, valid_lengths):
    heads = gate_logit.shape[0]
    seg, width = q.shape
    hd = width // heads
    nseq, nhead = lax.axis_size("seq"), lax.axis_size("head")
    wcols = out_weight.shape[1]
    per = nseq // nhead
    span = nseq // 2
    state = (heads, hd + EXT, hd)
    dma = pltpu.SemaphoreType.DMA
    smem = pl.BlockSpec(memory_space=pltpu.SMEM)
    vmem = pl.BlockSpec(memory_space=pltpu.VMEM)
    return pl.pallas_call(
        functools.partial(kernel, nseq, nhead, heads),
        out_shape=[jax.ShapeDtypeStruct((seg, width), BF16)] * 4,
        in_specs=[smem] * 3 + [vmem] * 5,
        out_specs=[vmem] * 4,
        scratch_shapes=[
            pltpu.VMEM((nseq, width, wcols), BF16),
            pltpu.VMEM((nhead, seg, wcols * per), BF16),
            pltpu.VMEM((nseq, seg, wcols), BF16),
            pltpu.VMEM((nseq, seg, wcols), BF16),
            pltpu.VMEM((heads, seg, seg), BF16),
            pltpu.VMEM((seg, width), F32),
            pltpu.VMEM((seg, width), BF16),
            pltpu.VMEM((seg, width), BF16),
            pltpu.VMEM((seg, width), F32),
            pltpu.VMEM((seg, width), F32),
            pltpu.VMEM((seg, width), F32),
            pltpu.VMEM((seg, width), BF16),
            pltpu.VMEM((seg, width), BF16),
            pltpu.VMEM(state, BF16),
            pltpu.VMEM(state, BF16),
            pltpu.VMEM((span - 1,) + state, BF16),
            pltpu.VMEM(state, BF16),
            pltpu.VMEM((span - 1,) + state, BF16),
            dma((span,)), dma((span,)), dma((nseq,)),
            dma((2, nhead)), dma((nhead,)),
            dma((span - 1,)), dma((span - 1,)), dma((span - 1,)), dma((span - 1,)),
            dma((2, nseq)), dma((2, nseq)), dma((2,)),
        ],
        compiler_params=pltpu.CompilerParams(
            collective_id=0, has_side_effects=True, vmem_limit_bytes=60 * 1024 * 1024
        ),
        cost_estimate=pl.CostEstimate(
            flops=4 * seg * width * wcols * nseq, bytes_accessed=18 * seg * width,
            transcendentals=0,
        ),
        name="layer",
    )(valid_lengths, document_ids, gate_logit, q, k, v, upstream, out_weight)


def solution(mesh):
    spec = P("seq", "head")
    return jax.shard_map(
        per_device,
        mesh=mesh,
        in_specs=(spec, spec, spec, spec, P("head", "seq"), P("head"), P(), P()),
        out_specs=(spec, spec, spec, spec),
        check_vma=False,
    )
```
